512 devices in a mesh: wide: 64 (over z, y), narrow: 8 (over x, core).
Axes of the slice: x: 4, y: 4, z: 16, core: 2. Of those that a mesh axis runs over, the one named last changes fastest.
Arguments:
- coeffs: bfloat16 [65536, 9216], P('wide', 'narrow'), may hold values from -6 to 6
- earlier: bfloat16 [65536, 2048], P('wide', 'narrow'), may hold values from -6 to 6
- inv_tiles: float32 [4, 128, 128], replicated, may hold values from -0.041666667 to 0.041666667
- piv_local: int32 [512], replicated, may hold values from 0 to 1023
- piv_owner: int32 [512, 1], replicated, may hold values from 0 to 63; in each aligned block of 512 rows (0 to 511, 512 to 1023, ...) at most 24 rows name the same one
Outputs:
- new_columns: float32 [65536, 512], P('wide', 'narrow')
The draws below stay inside these ranges and needn't reach their ends.
Inputs may be any that keep to these rules, and one draw needn't show every extreme that they name: `piv_owner`: each index of wide owns at most 24 of the 512 pivots, and some index owns exactly 24.
All inputs are finite; a program needn't handle non-finite values.
Results may differ from the reference program's by a relative error of at most 0.0003.
Values may be sent and summed in bfloat16 or wider, within the bound.
A program may use at most 64 MiB of HBM per device.

```python
import math
import jax
import jax.numpy as jnp
import numpy as np
from jax import lax

NOCC = 9216
PANEL = 512
BLOCK = 128
ROWS_DEV = 1024
KPREV = 2048
NBLK = 4
NAO = 65536
CAP = 24
N_WIDE = 64


def draw_inv_tiles(key, part):
    key_diag = jax.random.fold_in(key, 11)
    key_off = jax.random.fold_in(key, 12)
    tile_scale = 1.0 / jnp.sqrt(jnp.float32(NOCC))
    identity = jnp.eye(BLOCK, dtype=jnp.float32)
    diag_vals = jnp.exp(jax.random.uniform(key_diag, (NBLK, BLOCK), jnp.float32, math.log(0.5), math.log(2.0)))
    spread = jax.random.truncated_normal(key_off, -4.0, 4.0, (NBLK, BLOCK, BLOCK), jnp.float32)
    offdiag = spread * (0.4 / math.sqrt(BLOCK)) * (1.0 - identity)
    return ((identity * diag_vals[:, :, None] + offdiag) * tile_scale).astype(jnp.float32)


def set_ends(values, stream_key, low, top_value):
    dims = values.shape
    spot = [jax.random.randint(jax.random.fold_in(stream_key, axis), (), 0, dims[axis]) for axis in range(len(dims))]
    values = values.at[tuple(spot)].set(low)
    longest = dims.index(max(dims))
    spot[longest] = (spot[longest] + 1) % dims[longest]
    return values.at[tuple(spot)].set(top_value)


def level_of(rng, shape, cuts, least, high):
    def one(dim, shards_of):
        heights = jax.random.uniform(jax.random.fold_in(jax.random.fold_in(rng, 6), dim), (shards_of,), jnp.float32, least / len(cuts), high / len(cuts))
        return jnp.repeat(jnp.exp(heights), shape[dim] // shards_of).reshape((-1,) + (1,) * (len(shape) - dim - 1))

    gain = one(*cuts[0])
    for cut in cuts[1:]:
        gain = gain * one(*cut)
    return gain


def assign_block(key, own, number, rows, number_of, top, bound, slope):
    order = jax.random.permutation(key, number_of)
    crowded, usual = portions_of(number_of, rows * top, bound, slope, True), portions_of(number_of, rows * top, bound, slope, False)
    places = jnp.arange(number_of)

    def named(sizes, rotation):
        used = int((sizes > 0).sum())
        fixed = max(1, used // 4)
        shifted = fixed + (places - fixed + rotation * (used - fixed)) % max(1, number_of - fixed)
        return jnp.zeros((number_of,), jnp.int32).at[order[jnp.where(places < fixed, places, shifted)]].set(jnp.asarray(sizes, jnp.int32))

    sizes = jnp.where(number % 4 == 0, named(crowded, number // 4), named(usual, number - number // 4 - 1))
    mixed = jax.random.permutation(jax.random.fold_in(own, 3), number_of)
    source_of, taker = mixed[0:number_of // 2 * 2:2], mixed[1:number_of // 2 * 2:2]
    room = jnp.minimum(sizes[source_of] - 1, bound - sizes[taker]) // 2
    room = jnp.where((source_of == order[0]) | (taker == order[0]) | (sizes[taker] == 0), 0, jnp.maximum(room, 0))
    shifted = jax.random.randint(jax.random.fold_in(own, 4), (number_of // 2,), 0, 1 << 20) % (room + 1)
    sizes = sizes.at[source_of].add(-shifted).at[taker].add(shifted)
    labels = jnp.searchsorted(jnp.cumsum(sizes), jnp.arange(rows * top), side="right").astype(jnp.int32)
    table = labels.reshape(top, rows).T
    table = table[jax.random.permutation(jax.random.fold_in(own, 1), rows)]
    rotation = jax.random.randint(jax.random.fold_in(own, 2), (rows, 1), 0, top)
    return jnp.take_along_axis(table, (jnp.arange(top)[None, :] + rotation) % top, axis=1)


def portions_of(amount, total, limit, skew, full):
    loads = [(1 << 20) // math.isqrt(rank ** skew) + 1 for rank in range(1, amount + 1)]
    largest = limit if full else min(limit, max(-(-total // amount), total * loads[0] // sum(loads)))
    least = 1 if total - largest >= amount - 1 else 0
    counts, rest = [largest] + [least] * (amount - 1), total - largest - least * (amount - 1)
    while rest > 0:
        free = [i for i in range(1, amount) if counts[i] < largest] or [i for i in range(1, amount) if counts[i] < limit]
        whole, remaining = sum([loads[i] for i in free]), rest
        for i in free:
            extra = min(limit - counts[i], max(1, remaining * loads[i] // whole), rest)
            counts[i] = counts[i] + extra
            rest = rest - extra
    return np.array(counts)


def normal_values(own_key, shape, scale, reach, split=(), kind=jnp.bfloat16):
    array = scale * jax.random.normal(own_key, shape, jnp.float32)
    if split:
        array = array * level_of(own_key, shape, split, -0.22, 0.18)
    return jnp.clip(array, -reach, reach).astype(kind)


def setup_inputs(seed: int = 0) -> dict:
    keys = jax.random.split(jax.random.key(seed), 6)
    coeffs = normal_values(keys[0], (NAO, NOCC), 1.0, 6.0, ((0, 64), (1, 8)))
    earlier = normal_values(keys[1], (NAO, KPREV), 1.0, 6.0, ((0, 64), (1, 8)))
    inv_tiles = draw_inv_tiles(jax.random.fold_in(keys[5], 71), 0)
    piv_local = set_ends(jax.random.randint(keys[3], (PANEL,), 0, ROWS_DEV), jax.random.fold_in(keys[3], 1), 0, ROWS_DEV - 1).astype(jnp.int32)
    piv_owner_keys = jax.random.split(jax.random.fold_in(keys[4], 1), PANEL // PANEL)
    piv_owner_turns = jax.random.permutation(jax.random.fold_in(keys[4], 3), PANEL // PANEL)
    piv_owner = jax.vmap(lambda own, number: assign_block(jax.random.fold_in(keys[4], 2), own, number, PANEL, N_WIDE, 1, CAP, 2))(piv_owner_keys, piv_owner_turns).reshape((PANEL, 1))
    return {"coeffs": coeffs, "earlier": earlier, "inv_tiles": inv_tiles, "piv_local": piv_local, "piv_owner": piv_owner}


def panel_factor(density, diag_block, inv_tiles):
    block_size = inv_tiles.shape[1]
    piv_parts = []
    new_parts = []
    for block_index in range(inv_tiles.shape[0]):
        low_edge = block_index * block_size
        high_edge = low_edge + block_size
        piv_rest = diag_block[:, low_edge:high_edge]
        new_rest = density[:, low_edge:high_edge]
        if block_index > 0:
            piv_left = jnp.concatenate(piv_parts, axis=1)
            new_left = jnp.concatenate(new_parts, axis=1)
            coupling = piv_left[low_edge:high_edge]
            piv_rest = piv_rest - jnp.dot(piv_left, coupling.T, precision=lax.Precision.HIGHEST)
            new_rest = new_rest - jnp.dot(new_left, coupling.T, precision=lax.Precision.HIGHEST)
        piv_parts.append(jnp.dot(piv_rest, inv_tiles[block_index], precision=lax.Precision.HIGHEST))
        new_parts.append(jnp.dot(new_rest, inv_tiles[block_index], precision=lax.Precision.HIGHEST))
    return jnp.concatenate(new_parts, axis=1)


def reference(coeffs, earlier, inv_tiles, piv_local, piv_owner):
    global_rows = (piv_owner[:, 0] * ROWS_DEV + piv_local).astype(jnp.int32)
    pivot_coeffs = coeffs[global_rows]
    pivot_earlier = earlier[global_rows]
    density = jnp.dot(coeffs, pivot_coeffs.T, preferred_element_type=jnp.float32)
    density = density - jnp.dot(earlier, pivot_earlier.T, preferred_element_type=jnp.float32)
    diag_block = density[global_rows]
    return panel_factor(density, diag_block, inv_tiles)
```

```python
import jax
import jax.numpy as jnp
from jax import lax
from jax.experimental import pallas as pl
from jax.experimental.pallas import tpu as pltpu
from jax.sharding import PartitionSpec as P

MESH = pl.DeviceIdType.MESH
F32 = jnp.float32
BF16 = jnp.bfloat16
HIGH = lax.Precision.HIGHEST

NPIV = 512
BLK = 128
NY = 4
NZ = 16
NX = 4
CAP = 24
SLOT = 32
GROUP = CAP * NY
PIECES = 3
QCOL = PIECES * 128
LOW = ((1, 0), (2, 0), (2, 1), (3, 0), (3, 1), (3, 2))
SKEW = 2


def dot(a, b, precision=None):
    return lax.dot_general(a, b, (((1,), (0,)), ((), ())), precision=precision, preferred_element_type=F32)


def dot_nt(a, b, precision=None):
    return lax.dot_general(a, b, (((1,), (1,)), ((), ())), precision=precision, preferred_element_type=F32)


def ones_where(cond):
    return jnp.where(cond, 1.0, 0.0).astype(F32)


def kernel(coeffs, earlier, inv, own_col, own_row, loc_row, out,
           sel, ygot, ring, rows, hot,
           diag, diag_core, diag_x, diag_all,
           part_send, part_mine, part_got, half_a, half_b, from_left, from_right,
           pack, got,
           y1s, y1r, zs, zr, y2s, y2r, dcs, dcr, dxs, dxr, dys, dyr, pcs, pcr, xas, xar, xbs, xbr, os_, or_):
    wide = lax.axis_index("wide")
    narrow = lax.axis_index("narrow")
    z, y = wide // NY, wide % NY
    x, core = narrow // 2, narrow % 2
    z_next, z_prev = (z + 1) % NZ, (z + NZ - 1) % NZ
    y_next, y_prev = (y + 1) % NY, (y + NY - 1) % NY
    x_next, x_prev, x_far = (x + 1) % NX, (x + 3) % NX, (x + 2) % NX

    def at(zz=z, yy=y, xx=x, cc=core):
        return {"wide": zz * NY + yy, "narrow": xx * 2 + cc}

    def remote(src, dst, send_sem, recv_sem, device):
        return pltpu.make_async_remote_copy(
            src_ref=src, dst_ref=dst, send_sem=send_sem, recv_sem=recv_sem,
            device_id=device, device_id_type=MESH)

    other = 1 - core
    ys = [(y + d) % NY for d in (1, 3, 2)]
    xs = [x_next, x_prev, x_far]

    barrier = pltpu.get_barrier_semaphore()
    peers = [at(zz=z_next), at(zz=z_prev), at(cc=other)]
    peers += [at(yy=v, cc=c) for v in ys for c in (core, other)]
    peers += [at(xx=v, cc=c) for v in xs for c in (core, other)]
    for peer in peers:
        pl.semaphore_signal(barrier, inc=1, device_id=peer, device_id_type=MESH)

    owners = own_row[...]
    owner_col = own_col[...]
    before = lax.broadcasted_iota(jnp.int32, (NPIV, NPIV), 0) < lax.broadcasted_iota(jnp.int32, (NPIV, NPIV), 1)
    same_owner = owner_col == owners
    slot_row = jnp.sum(ones_where(before & same_owner), axis=0, keepdims=True)
    slots = lax.broadcasted_iota(jnp.int32, (SLOT, NPIV), 0).astype(F32)
    held = (slots == slot_row) & (owners == wide)
    place = jnp.sum(jnp.where(held, loc_row[...].astype(F32) + 1.0, 0.0), axis=1, keepdims=True) - 1.0
    pick = ones_where(lax.broadcasted_iota(jnp.int32, (SLOT, 1024), 1).astype(F32) == place).astype(BF16)
    n_coeff, n_early = coeffs.shape[-1], earlier.shape[-1]
    sel[:, :n_coeff] = dot(pick, coeffs[...].reshape(1024, n_coeff)).astype(BF16)
    sel[:, n_coeff:n_coeff + n_early] = dot(pick, earlier[...].reshape(1024, n_early)).astype(BF16)
    rest = NY * QCOL - n_coeff - n_early
    sel[:, n_coeff + n_early:] = jnp.zeros((SLOT, rest), BF16)

    pl.semaphore_wait(barrier, len(peers))

    def quarter(v):
        return pl.ds(pl.multiple_of(v * QCOL, 128), QCOL)

    spread = [remote(sel.at[:, quarter(v)], ygot.at[y], y1s.at[i], y1r.at[i], at(yy=v)) for i, v in enumerate(ys)]
    for copy in spread:
        copy.start()
    ygot[y] = sel[:, quarter(y)]

    z_row, z_col = owners // NY, owner_col // NY
    same_z = z_col == z_row
    rank_row = jnp.sum(ones_where(before & same_z), axis=0, keepdims=True)
    after = lax.broadcasted_iota(jnp.int32, (NPIV, NPIV), 1) < lax.broadcasted_iota(jnp.int32, (NPIV, NPIV), 0)
    rank_col = jnp.sum(ones_where(after & same_z), axis=1, keepdims=True)
    slot_col = jnp.sum(ones_where(after & same_owner), axis=1, keepdims=True)
    ranks = lax.broadcasted_iota(jnp.int32, (GROUP, NPIV), 0).astype(F32)
    to_rank = ones_where((ranks == rank_row) & (z_row == z)).astype(BF16)
    source = (owner_col % NY * SLOT).astype(F32) + slot_col
    from_slot = ones_where((lax.broadcasted_iota(jnp.int32, (NPIV, NY * SLOT), 1).astype(F32) == source) & (z_col == z)).astype(BF16)
    compact = dot(to_rank, from_slot).astype(BF16)
    target = (z_col * GROUP).astype(F32) + rank_col
    hot[...] = ones_where(lax.broadcasted_iota(jnp.int32, (NPIV, NZ * GROUP), 1).astype(F32) == target).astype(BF16)

    for copy in spread:
        copy.wait_recv()
    chunk = dot(compact, ygot[...].reshape(NY * SLOT, QCOL)).astype(BF16)

    def chunk_rows(v):
        return pl.ds(pl.multiple_of(v * GROUP, 16), GROUP)

    for g in range(PIECES):
        ring[g, chunk_rows(z), :] = chunk[:, g * 128:(g + 1) * 128]

    def ring_copy(way, step, g):
        origin = (z - (step - 1) + NZ) % NZ if way == 0 else (z + (step - 1)) % NZ
        ref = ring.at[g, chunk_rows(origin), :]
        return remote(ref, ref, zs.at[way, step - 1, g], zr.at[way, step - 1, g], at(zz=z_next if way == 0 else z_prev))

    def steps_of(way, g):
        longer = 0 if g % 2 == 0 else 1
        return NZ // 2 if way == longer else NZ // 2 - 1

    copies = {(way, s, g): ring_copy(way, s, g) for g in range(PIECES) for way in (0, 1) for s in range(1, steps_of(way, g) + 1)}

    def column(v, g):
        return pl.ds(pl.multiple_of(v * QCOL + g * 128, 128), 128)

    def whole_copy(way, g):
        ref = rows.at[:, column(y, g)]
        return remote(ref, ref, y2s.at[way, g], y2r.at[way, g], at(yy=y_next if way == 0 else y_prev))

    def pass_on(way, g):
        ref = rows.at[pl.ds(way * 256, 256), column(y_prev if way == 0 else y_next, g)]
        return remote(ref, ref, y2s.at[2 + way, g], y2r.at[2 + way, g], at(yy=y_next if way == 0 else y_prev))

    whole = {(way, g): whole_copy(way, g) for way in (0, 1) for g in range(PIECES)}
    passed = {(way, g): pass_on(way, g) for way in (0, 1) for g in range(PIECES)}

    def finish_piece(g):
        for way in (0, 1):
            copies[way, steps_of(way, g), g].wait_recv()
        rows[:, column(y, g)] = dot(hot[...], ring[g]).astype(BF16)
        for way in (0, 1):
            whole[way, g].start()

    for tick in range(1, NZ // 2 + 1 + SKEW * (PIECES - 1) + 1):
        for g in range(PIECES):
            step = tick - SKEW * g
            for way in (0, 1):
                if 1 <= step <= steps_of(way, g):
                    if step > 1:
                        copies[way, step - 1, g].wait_recv()
                    copies[way, step, g].start()
            if step == NZ // 2 + 1:
                finish_piece(g)
    for g in range(PIECES):
        for way in (0, 1):
            whole[way, g].wait_recv()
            passed[way, g].start()
    for g in range(PIECES):
        for way in (0, 1):
            passed[way, g].wait_recv()

    def pivots(low, high):
        return rows[low:high, :n_coeff], rows[low:high, n_coeff:n_coeff + n_early]

    for b in (1, 2, 3):
        left_c, left_e = pivots(b * BLK, (b + 1) * BLK)
        right_c, right_e = pivots(0, b * BLK)
        value = dot_nt(left_c, right_c) - dot_nt(left_e, right_e)
        for c in range(b):
            diag[LOW.index((b, c))] = value[:, c * BLK:(c + 1) * BLK]

    to_core = remote(diag.at[pl.ds(other * 3, 3)], diag_core, dcs, dcr, at(cc=other))
    to_core.start()

    piv_c, piv_e = pivots(0, NPIV)

    def partial(c):
        left_c = coeffs[:, c].reshape(NX * BLK, n_coeff)
        left_e = earlier[:, c].reshape(NX * BLK, n_early)
        return (dot_nt(left_c, piv_c) - dot_nt(left_e, piv_e)).reshape(NX, BLK, NPIV)

    part_send[...] = partial(other)
    order = [x_far, x_next, x_prev, x]
    part_copies = [remote(part_send.at[v], part_got.at[v], pcs.at[i], pcr.at[i], at(cc=other)) for i, v in enumerate(order)]
    for copy in part_copies:
        copy.start()

    def quarter_rows(v):
        return pl.ds(pl.multiple_of(v * 32, 32), 32)

    to_core.wait_recv()
    diag_x[x] = diag[pl.ds(core * 3, 3), quarter_rows(y)] + diag_core[:, quarter_rows(y)]
    diag_xs = [remote(diag_x.at[x], diag_x.at[x], dxs.at[i], dxr.at[i], at(xx=v)) for i, v in enumerate(xs)]
    for copy in diag_xs:
        copy.start()

    part_mine[...] = partial(core)

    for copy in diag_xs:
        copy.wait()
    diag_all[pl.ds(core * 3, 3), quarter_rows(y)] = diag_x[0] + diag_x[1] + diag_x[2] + diag_x[3]
    spot = diag_all.at[pl.ds(core * 3, 3), quarter_rows(y)]
    kin = [at(yy=v, cc=c) for v in ys for c in (core, other)] + [at(cc=other)]
    diag_ys = [remote(spot, spot, dys.at[i], dyr.at[i], who) for i, who in enumerate(kin)]
    for copy in diag_ys:
        copy.start()

    for v, copy in zip(order, part_copies):
        copy.wait_recv()
        part_mine[v] = part_mine[v] + part_got[v]
        if v is x_far:
            first_a = remote(part_mine.at[x_far, pl.ds(0, 64)], half_a, xas.at[0], xar.at[0], at(xx=x_next))
            first_b = remote(part_mine.at[x_far, pl.ds(64, 64)], half_b, xas.at[1], xar.at[1], at(xx=x_prev))
            first_a.start()
            first_b.start()
    next_now = remote(part_mine.at[x_next, pl.ds(64, 64)], from_left.at[pl.ds(64, 64)], xbs.at[0], xbr.at[0], at(xx=x_next))
    prev_now = remote(part_mine.at[x_prev, pl.ds(0, 64)], from_right.at[pl.ds(0, 64)], xbs.at[1], xbr.at[1], at(xx=x_prev))
    next_now.start()
    prev_now.start()
    first_a.wait_recv()
    part_mine[x_next, 0:64, :] = part_mine[x_next, 0:64, :] + half_a[...]
    next_then = remote(part_mine.at[x_next, pl.ds(0, 64)], from_left.at[pl.ds(0, 64)], xbs.at[2], xbr.at[2], at(xx=x_next))
    next_then.start()
    first_b.wait_recv()
    part_mine[x_prev, 64:128, :] = part_mine[x_prev, 64:128, :] + half_b[...]
    prev_then = remote(part_mine.at[x_prev, pl.ds(64, 64)], from_right.at[pl.ds(64, 64)], xbs.at[3], xbr.at[3], at(xx=x_prev))
    prev_then.start()

    for copy in diag_ys:
        copy.wait()
    low = {}
    for c in range(3):
        below = list(range(c + 1, 4))
        rest_rows = jnp.concatenate([diag_all[LOW.index((b, c))] for b in below], axis=0)
        for d in range(c):
            rest_rows = rest_rows - dot_nt(jnp.concatenate([low[b, d] for b in below], axis=0), low[c, d], HIGH)
        solved = dot(rest_rows, inv[c], HIGH)
        for i, b in enumerate(below):
            low[b, c] = solved[i * BLK:(i + 1) * BLK]

    for copy in (next_now, prev_now, next_then, prev_then):
        copy.wait_recv()
    density = part_mine[x] + from_left[...] + from_right[...]
    new = []
    outs = []
    for b in range(4):
        rest_cols = density[:, b * BLK:(b + 1) * BLK]
        for d in range(b):
            rest_cols = rest_cols - dot_nt(new[d], low[b, d], HIGH)
        value = dot(rest_cols, inv[b], HIGH)
        new.append(value)
        pack[2 * b] = jnp.concatenate([value[0:64, 0:64], value[64:128, 0:64]], axis=1)
        pack[2 * b + 1] = jnp.concatenate([value[0:64, 64:128], value[64:128, 64:128]], axis=1)
    home = [(x, other)] + [(v, c) for v in xs for c in (core, other)]
    for i, (xx, cc) in enumerate(home):
        copy = remote(pack.at[xx * 2 + cc], got.at[narrow], os_.at[i], or_.at[i], at(xx=xx, cc=cc))
        copy.start()
        outs.append(copy)
    got[narrow] = pack[narrow]
    for copy in outs:
        copy.wait_recv()
    for n in range(2 * NX):
        value = got[n]
        out[n * BLK:n * BLK + 64, :] = value[:, 0:64]
        out[n * BLK + 64:(n + 1) * BLK, :] = value[:, 64:128]

    for copy in spread + list(copies.values()) + list(whole.values()) + list(passed.values()):
        copy.wait_send()
    for copy in [to_core, first_a, first_b, next_now, prev_now, next_then, prev_then] + part_copies + outs:
        copy.wait_send()


def on_device(coeffs, earlier, inv_tiles, piv_local, piv_owner):
    n_coeff, n_early = coeffs.shape[1], earlier.shape[1]
    dma = pltpu.SemaphoreType.DMA
    vmem = pltpu.VMEM
    return pl.pallas_call(
        kernel,
        out_shape=jax.ShapeDtypeStruct((1024, NPIV // (2 * NX)), F32),
        in_specs=[pl.BlockSpec(memory_space=pltpu.VMEM)] * 6,
        out_specs=pl.BlockSpec(memory_space=pltpu.VMEM),
        scratch_shapes=[
            vmem((SLOT, NY * QCOL), BF16),
            vmem((NY, SLOT, QCOL), BF16),
            vmem((PIECES, NZ * GROUP, 128), BF16),
            vmem((NPIV, NY * QCOL), BF16),
            vmem((NPIV, NZ * GROUP), BF16),
            vmem((6, BLK, BLK), F32),
            vmem((3, BLK, BLK), F32),
            vmem((NX, 3, 32, BLK), F32),
            vmem((6, BLK, BLK), F32),
            vmem((NX, BLK, NPIV), F32),
            vmem((NX, BLK, NPIV), F32),
            vmem((NX, BLK, NPIV), F32),
            vmem((64, NPIV), F32),
            vmem((64, NPIV), F32),
            vmem((BLK, NPIV), F32),
            vmem((BLK, NPIV), F32),
            vmem((2 * NX, 64, BLK), F32),
            vmem((2 * NX, 64, BLK), F32),
            dma((3,)), dma((3,)),
            dma((2, NZ // 2, PIECES)), dma((2, NZ // 2, PIECES)),
            dma((4, PIECES)), dma((4, PIECES)),
            dma, dma,
            dma((3,)), dma((3,)),
            dma((7,)), dma((7,)),
            dma((4,)), dma((4,)),
            dma((2,)), dma((2,)),
            dma((4,)), dma((4,)),
            dma((7,)), dma((7,)),
        ],
        compiler_params=pltpu.CompilerParams(
            collective_id=0, has_side_effects=True, vmem_limit_bytes=56 * 1024 * 1024),
        cost_estimate=pl.CostEstimate(flops=4_000_000_000, bytes_accessed=4_000_000, transcendentals=0),
    )(coeffs.reshape(NX, 2, BLK, n_coeff), earlier.reshape(NX, 2, BLK, n_early), inv_tiles,
      piv_owner, piv_owner.reshape(1, NPIV), piv_local.reshape(1, NPIV))


def solution(mesh):
    return jax.shard_map(
        on_device,
        mesh=mesh,
        in_specs=(P("wide", "narrow"), P("wide", "narrow"), P(), P(), P()),
        out_specs=P("wide", "narrow"),
        check_vma=False,
    )
```

```python
import jax
import jax.numpy as jnp
from jax import lax
from jax.experimental import pallas as pl
from jax.experimental.pallas import tpu as pltpu
from jax.sharding import PartitionSpec as P

MESH = pl.DeviceIdType.MESH
F32 = jnp.float32
BF16 = jnp.bfloat16
HIGH = lax.Precision.HIGHEST

NPIV = 512
BLK = 128
NBLK = 4
NY = 4
NZ = 16
NX = 4
CAP = 24
SLOT = 32
GROUP = CAP * NY
PIECES = 3
QCOL = PIECES * 128
LOW = ((1, 0), (2, 0), (2, 1), (3, 0), (3, 1), (3, 2))
STEPS = NZ // 4


def dot(a, b, precision=None):
    return lax.dot_general(a, b, (((1,), (0,)), ((), ())), precision=precision, preferred_element_type=F32)


def dot_nt(a, b, precision=None):
    return lax.dot_general(a, b, (((1,), (1,)), ((), ())), precision=precision, preferred_element_type=F32)


def ones_where(cond):
    return jnp.where(cond, 1.0, 0.0).astype(F32)


def iota(shape, dim):
    return lax.broadcasted_iota(jnp.int32, shape, dim)


def kernel(coeffs_in, earlier_in, inv, own_row, loc_row, out,
           coeffs, earlier, sel, ygot, ring, rows, hot,
           diag, diag_core, diag_sum, diag_x, diag_y, diag_all,
           part_send, part_got, part_sum, x_got, made, got,
           ins, y1s, y1r, zs, zr, y2s, y2r, d1s, d1r, d2s, d2r, d3s, d3r, d4s, d4r, d5s, d5r,
           pcs, pcr, xas, xar, os_, or_):
    wide = lax.axis_index("wide")
    narrow = lax.axis_index("narrow")
    z, y = wide // NY, wide % NY
    x, core = narrow // 2, narrow % 2
    other = 1 - core
    ys = [(y + d) % NY for d in (1, 3, 2)]
    xs = [(x + d) % NX for d in (1, 3, 2)]

    def at(zz=z, yy=y, xx=x, cc=core):
        return {"wide": zz * NY + yy, "narrow": xx * 2 + cc}

    def remote(src, dst, send_sem, recv_sem, device):
        return pltpu.make_async_remote_copy(
            src_ref=src, dst_ref=dst, send_sem=send_sem, recv_sem=recv_sem,
            device_id=device, device_id_type=MESH)

    def start(copies):
        for copy in copies:
            copy.start()

    def arrive(copies):
        for copy in copies:
            copy.wait_recv()

    sent = []

    barrier = pltpu.get_barrier_semaphore()
    peers = [at(zz=(z + d) % NZ) for d in (1, 2, NZ - 1, NZ - 2)] + [at(cc=other)]
    peers += [at(yy=v) for v in ys]
    peers += [at(xx=v, cc=c) for v in xs for c in (core, other)]
    for peer in peers:
        pl.semaphore_signal(barrier, inc=1, device_id=peer, device_id_type=MESH)
    fetch = [pltpu.make_async_copy(coeffs_in, coeffs, ins.at[0]), pltpu.make_async_copy(earlier_in, earlier, ins.at[1])]
    start(fetch)

    owners = own_row[...]
    up, along = iota((NPIV, NPIV), 0), iota((NPIV, NPIV), 1)
    owner_col = jnp.sum(jnp.where(up == along, owners.astype(F32), 0.0), axis=1, keepdims=True).astype(jnp.int32)
    before, after = up < along, along < up
    same_owner = owner_col == owners
    slot_row = jnp.sum(ones_where(before & same_owner), axis=0, keepdims=True)
    held = (iota((SLOT, NPIV), 0).astype(F32) == slot_row) & (owners == wide)
    place = jnp.sum(jnp.where(held, loc_row[...].astype(F32) + 1.0, 0.0), axis=1, keepdims=True) - 1.0
    pick = ones_where(iota((SLOT, 1024), 1).astype(F32) == place).astype(BF16)

    z_row, z_col = owners // NY, owner_col // NY
    same_z = z_col == z_row
    rank_row = jnp.sum(ones_where(before & same_z), axis=0, keepdims=True)
    rank_col = jnp.sum(ones_where(after & same_z), axis=1, keepdims=True)
    slot_col = jnp.sum(ones_where(after & same_owner), axis=1, keepdims=True)
    to_rank = ones_where((iota((GROUP, NPIV), 0).astype(F32) == rank_row) & (z_row == z)).astype(BF16)
    source = (owner_col % NY * SLOT).astype(F32) + slot_col
    from_slot = ones_where((iota((NPIV, NY * SLOT), 1).astype(F32) == source) & (z_col == z)).astype(BF16)
    compact = dot(to_rank, from_slot).astype(BF16)
    target = (z_col * GROUP).astype(F32) + rank_col
    hot[...] = ones_where(iota((NPIV, NZ * GROUP), 1).astype(F32) == target).astype(BF16)

    n_coeff, n_early = coeffs.shape[-1], earlier.shape[-1]
    for copy in fetch:
        copy.wait()
    sel[:, :n_coeff] = dot(pick, coeffs[...].reshape(1024, n_coeff)).astype(BF16)
    sel[:, n_coeff:n_coeff + n_early] = dot(pick, earlier[...].reshape(1024, n_early)).astype(BF16)
    rest = NY * QCOL - n_coeff - n_early
    sel[:, n_coeff + n_early:] = jnp.zeros((SLOT, rest), BF16)

    pl.semaphore_wait(barrier, len(peers))

    def quarter(v):
        return pl.ds(pl.multiple_of(v * QCOL, 128), QCOL)

    spread = [remote(sel.at[:, quarter(v)], ygot.at[y], y1s.at[i], y1r.at[i], at(yy=v)) for i, v in enumerate(ys)]
    start(spread)
    sent += spread
    ygot[y] = sel[:, quarter(y)]
    arrive(spread)
    chunk = dot(compact, ygot[...].reshape(NY * SLOT, QCOL)).astype(BF16)

    def chunk_rows(v):
        return pl.ds(pl.multiple_of(v * GROUP, 16), GROUP)

    for g in range(PIECES):
        ring[g, chunk_rows(z), :] = chunk[:, g * 128:(g + 1) * 128]

    def ring_copy(way, step, g, far):
        sign = 1 if way == 0 else NZ - 1
        origin = (z + (NZ - sign) * 2 * (step - 1)) % NZ
        ref = ring.at[g, chunk_rows(origin), :]
        return remote(ref, ref, zs.at[way, step - 1, g, far], zr.at[way, step - 1, g, far],
                      at(zz=(z + sign * (1 + far)) % NZ))

    hops = {}
    for g in range(PIECES):
        for way in (0, 1):
            for step in range(1, STEPS + 1):
                hops[way, step, g, 0] = ring_copy(way, step, g, 0)
                if step < STEPS or way == g % 2:
                    hops[way, step, g, 1] = ring_copy(way, step, g, 1)
    for step in range(1, STEPS + 1):
        for g in range(PIECES):
            for way in (0, 1):
                if step > 1:
                    hops[way, step - 1, g, 1].wait_recv()
                for far in (1, 0):
                    if (way, step, g, far) in hops:
                        hops[way, step, g, far].start()
    sent += list(hops.values())

    def column(v, g):
        return pl.ds(pl.multiple_of(v * QCOL + g * 128, 128), 128)

    for g in range(PIECES):
        for (way, step, gg, far), copy in hops.items():
            if gg == g and (far == 0 or step == STEPS):
                copy.wait_recv()
        rows[:, column(y, g)] = dot(hot[...], ring[g]).astype(BF16)

    def y_send(b):
        ref = rows.at[pl.ds(b * BLK, BLK), quarter(y)]
        copies = [remote(ref, ref, y2s.at[b, i], y2r.at[b, i], at(yy=v)) for i, v in enumerate(ys)]
        start(copies)
        return copies

    y_copies = [y_send(0), y_send(1)]

    mine = rows[:, quarter(y)]
    gain = jnp.where(y == NY - 1, -1.0, 1.0).astype(F32)
    for b in (1, 2, 3):
        value = dot_nt(mine[b * BLK:(b + 1) * BLK], mine[:b * BLK]) * gain
        for c in range(b):
            diag[LOW.index((b, c))] = value[:, c * BLK:(c + 1) * BLK]
    d1 = remote(diag.at[pl.ds(other * 3, 3)], diag_core, d1s, d1r, at(cc=other))
    d1.start()

    def few_rows(v):
        return pl.ds(pl.multiple_of(v * 32, 32), 32)

    d1.wait_recv()
    diag_sum[...] = diag[pl.ds(core * 3, 3)] + diag_core[...]
    d2 = [remote(diag_sum.at[:, few_rows(v)], diag_x.at[x], d2s.at[i], d2r.at[i], at(xx=v)) for i, v in enumerate(xs)]
    start(d2)
    diag_x[x] = diag_sum[:, few_rows(x)]
    y_copies += [y_send(2), y_send(3)]
    sent += [d1] + d2
    for copies in y_copies:
        sent += copies

    def density(b, c):
        block = rows[b * BLK:(b + 1) * BLK, :]
        left = dot_nt(block[:, :n_coeff], coeffs[:, c].reshape(NX * BLK, n_coeff))
        return left - dot_nt(block[:, n_coeff:n_coeff + n_early], earlier[:, c].reshape(NX * BLK, n_early))

    core_copies = []

    def to_core(b):
        arrive(y_copies[b])
        part_send[b] = density(b, other)
        copy = remote(part_send.at[b], part_got.at[b], pcs.at[b], pcr.at[b], at(cc=other))
        copy.start()
        core_copies.append(copy)
        part_sum[b] = density(b, core)

    def chip(v):
        return pl.ds(pl.multiple_of(v * BLK, BLK), BLK)

    x_copies = []

    def to_x(b):
        core_copies[b].wait_recv()
        part_sum[b] = part_sum[b] + part_got[b]
        copies = [remote(part_sum.at[b, :, chip(v)], x_got.at[b, i], xas.at[b, i], xar.at[b, i], at(xx=v))
                  for i, v in enumerate(xs)]
        start(copies)
        x_copies.append(copies)

    low = {}
    new = []
    home = [(x, other)] + [(v, c) for v in xs for c in (core, other)]

    def finish(b):
        arrive(x_copies[b])
        rest_rows = part_sum[b, :, chip(x)] + x_got[b, 0] + x_got[b, 1] + x_got[b, 2]
        for d in range(b):
            rest_rows = rest_rows - dot(low[b, d], new[d], HIGH)
        value = dot(inv[b].T, rest_rows, HIGH)
        new.append(value)
        made[b] = value
        for c in (0, 1):
            @pl.when((x != b) | (core != c))
            def _():
                out_copy(b, c).start()

            @pl.when((x == b) & (core == c))
            def _():
                got[:, chip(narrow)] = value[c * 64:(c + 1) * 64]

    def out_copy(b, c):
        return remote(made.at[b, pl.ds(c * 64, 64)], got.at[:, chip(narrow)], os_.at[b, c], or_.at[narrow], at(xx=b, cc=c))

    to_core(0)
    arrive(d2)
    diag_y[y] = diag_x[0] + diag_x[1] + diag_x[2] + diag_x[3]
    d3 = [remote(diag_y.at[y], diag_y.at[y], d3s.at[i], d3r.at[i], at(yy=v)) for i, v in enumerate(ys)]
    start(d3)
    to_x(0)
    to_core(1)
    to_x(1)
    arrive(d3)
    diag_all[pl.ds(core * 3, 3), few_rows(x)] = diag_y[0] + diag_y[1] + diag_y[2] + diag_y[3]
    spot = diag_all.at[pl.ds(core * 3, 3), few_rows(x)]
    d4 = [remote(spot, spot, d4s.at[i], d4r.at[i], at(xx=v)) for i, v in enumerate(xs)]
    start(d4)
    to_core(2)
    to_x(2)
    finish(0)
    arrive(d4)
    half = diag_all.at[pl.ds(core * 3, 3)]
    d5 = remote(half, half, d5s, d5r, at(cc=other))
    d5.start()
    to_core(3)
    to_x(3)
    d5.wait_recv()

    for c in range(3):
        below = list(range(c + 1, 4))
        rest_rows = jnp.concatenate([diag_all[LOW.index((b, c))] for b in below], axis=0)
        for d in range(c):
            rest_rows = rest_rows - dot_nt(jnp.concatenate([low[b, d] for b in below], axis=0), low[c, d], HIGH)
        solved = dot(rest_rows, inv[c], HIGH)
        for i, b in enumerate(below):
            low[b, c] = solved[i * BLK:(i + 1) * BLK]
    for b in (1, 2, 3):
        finish(b)

    for xx, cc in home:
        source_n = xx * 2 + cc
        remote(made.at[0, pl.ds(0, 64)], got.at[:, chip(source_n)], os_.at[0, 0], or_.at[source_n], at(xx=xx, cc=cc)).wait_recv()
    out[...] = got[...]

    for b in range(NBLK):
        for c in (0, 1):
            @pl.when((x != b) | (core != c))
            def _():
                out_copy(b, c).wait_send()
    sent += d3 + d4 + [d5] + core_copies
    for copies in x_copies:
        sent += copies
    for copy in sent:
        copy.wait_send()


def on_device(coeffs, earlier, inv_tiles, piv_local, piv_owner):
    n_coeff, n_early = coeffs.shape[1], earlier.shape[1]
    dma = pltpu.SemaphoreType.DMA
    vmem = pltpu.VMEM
    in_vmem = pl.BlockSpec(memory_space=pltpu.VMEM)
    anywhere = pl.BlockSpec(memory_space=pl.ANY)
    result = pl.pallas_call(
        kernel,
        out_shape=jax.ShapeDtypeStruct((NPIV // (2 * NX), 1024), F32),
        in_specs=[anywhere, anywhere, in_vmem, in_vmem, in_vmem],
        out_specs=in_vmem,
        scratch_shapes=[
            vmem((NX, 2, BLK, n_coeff), BF16),
            vmem((NX, 2, BLK, n_early), BF16),
            vmem((SLOT, NY * QCOL), BF16),
            vmem((NY, SLOT, QCOL), BF16),
            vmem((PIECES, NZ * GROUP, 128), BF16),
            vmem((NPIV, NY * QCOL), BF16),
            vmem((NPIV, NZ * GROUP), BF16),
            vmem((6, BLK, BLK), F32),
            vmem((3, BLK, BLK), F32),
            vmem((3, BLK, BLK), F32),
            vmem((NX, 3, 32, BLK), F32),
            vmem((NY, 3, 32, BLK), F32),
            vmem((6, BLK, BLK), F32),
            vmem((NBLK, BLK, NX * BLK), F32),
            vmem((NBLK, BLK, NX * BLK), F32),
            vmem((NBLK, BLK, NX * BLK), F32),
            vmem((NBLK, 3, BLK, BLK), F32),
            vmem((NBLK, BLK, BLK), F32),
            vmem((64, 1024), F32),
            dma((2,)),
            dma((3,)), dma((3,)),
            dma((2, STEPS, PIECES, 2)), dma((2, STEPS, PIECES, 2)),
            dma((NBLK, 3)), dma((NBLK, 3)),
            dma, dma,
            dma((3,)), dma((3,)),
            dma((3,)), dma((3,)),
            dma((3,)), dma((3,)),
            dma, dma,
            dma((NBLK,)), dma((NBLK,)),
            dma((NBLK, 3)), dma((NBLK, 3)),
            dma((NBLK, 2)), dma((2 * NX,)),
        ],
        compiler_params=pltpu.CompilerParams(
            collective_id=0, has_side_effects=True, vmem_limit_bytes=56 * 1024 * 1024),
        cost_estimate=pl.CostEstimate(flops=4_000_000_000, bytes_accessed=4_000_000, transcendentals=0),
    )(coeffs.reshape(NX, 2, BLK, n_coeff), earlier.reshape(NX, 2, BLK, n_early), inv_tiles,
      piv_owner.reshape(1, NPIV), piv_local.reshape(1, NPIV))
    return result.T


def solution(mesh):
    return jax.shard_map(
        on_device,
        mesh=mesh,
        in_specs=(P("wide", "narrow"), P("wide", "narrow"), P(), P(), P()),
        out_specs=P("wide", "narrow"),
        check_vma=False,
    )
```

```python
import jax
import jax.numpy as jnp
from jax import lax
from jax.experimental import pallas as pl
from jax.experimental.pallas import tpu as pltpu
from jax.sharding import PartitionSpec as P

MESH = pl.DeviceIdType.MESH
F32 = jnp.float32
BF16 = jnp.bfloat16
HIGH = lax.Precision.HIGHEST

NPIV = 512
BLK = 128
NBLK = 4
NY = 4
NZ = 16
NX = 4
CAP = 24
SLOT = 32
GROUP = CAP * NY
QCOL = 384
PARTS = ((0, 128), (128, 256))
LAG = (0, 0)
LOW = ((1, 0), (2, 0), (2, 1), (3, 0), (3, 1), (3, 2))
CHUNK = 64
WINDOW = 3
STEPS = NZ // 4


def dot(a, b, precision=None):
    return lax.dot_general(a, b, (((1,), (0,)), ((), ())), precision=precision, preferred_element_type=F32)


def dot_nt(a, b, precision=None):
    return lax.dot_general(a, b, (((1,), (1,)), ((), ())), precision=precision, preferred_element_type=F32)


def ones_where(cond):
    return jnp.where(cond, 1.0, 0.0).astype(F32)


def iota(shape, dim):
    return lax.broadcasted_iota(jnp.int32, shape, dim)


def kernel(coeffs_in, earlier_in, inv, own_row, loc_row, out,
           coeffs, earlier, inv_t, sel, ygot, ring_a, ring_b, rows, hot,
           diag, diag_core, diag_sum, diag_x, diag_y, diag_all,
           part_send, part_got, part_sum, x_got, made,
           ins, y1s, y1r, zs, zr, y2s, y2r, d1s, d1r, d2s, d2r, d3s, d3r, d4s, d4r, d5s, d5r,
           pcs, pcr, xas, xar, os_, or_):
    wide = lax.axis_index("wide")
    narrow = lax.axis_index("narrow")
    z, y = wide // NY, wide % NY
    x, core = narrow // 2, narrow % 2
    other = 1 - core
    ys = [(y + d) % NY for d in (1, 3, 2)]
    xs = [(x + d) % NX for d in (1, 3, 2)]

    def at(zz=z, yy=y, xx=x, cc=core):
        return {"wide": zz * NY + yy, "narrow": xx * 2 + cc}

    def remote(src, dst, send_sem, recv_sem, device):
        return pltpu.make_async_remote_copy(
            src_ref=src, dst_ref=dst, send_sem=send_sem, recv_sem=recv_sem,
            device_id=device, device_id_type=MESH)

    def start(copies):
        for copy in copies:
            copy.start()

    def arrive(copies):
        for copy in copies:
            copy.wait_recv()

    sent = []

    barrier = pltpu.get_barrier_semaphore()
    peers = [at(zz=(z + d) % NZ) for d in (1, 2, NZ - 1, NZ - 2)] + [at(cc=other)]
    peers += [at(yy=v) for v in ys]
    peers += [at(xx=v, cc=c) for v in xs for c in (core, other)]
    for peer in peers:
        pl.semaphore_signal(barrier, inc=1, device_id=peer, device_id_type=MESH)
    fetch = [pltpu.make_async_copy(coeffs_in, coeffs, ins.at[0]), pltpu.make_async_copy(earlier_in, earlier, ins.at[1])]
    start(fetch)

    owners = own_row[...]
    up, along = iota((NPIV, NPIV), 0), iota((NPIV, NPIV), 1)
    owner_col = jnp.sum(jnp.where(up == along, owners.astype(F32), 0.0), axis=1, keepdims=True).astype(jnp.int32)
    before, after = up < along, along < up
    same_owner = owner_col == owners
    slot_row = jnp.sum(ones_where(before & same_owner), axis=0, keepdims=True)
    held = (iota((SLOT, NPIV), 0).astype(F32) == slot_row) & (owners == wide)
    place = jnp.sum(jnp.where(held, loc_row[...].astype(F32) + 1.0, 0.0), axis=1, keepdims=True) - 1.0
    pick = ones_where(iota((SLOT, 1024), 1).astype(F32) == place).astype(BF16)

    z_row, z_col = owners // NY, owner_col // NY
    same_z = z_col == z_row
    rank_row = jnp.sum(ones_where(before & same_z), axis=0, keepdims=True)
    rank_col = jnp.sum(ones_where(after & same_z), axis=1, keepdims=True)
    slot_col = jnp.sum(ones_where(after & same_owner), axis=1, keepdims=True)
    to_rank = ones_where((iota((GROUP, NPIV), 0).astype(F32) == rank_row) & (z_row == z)).astype(BF16)
    source = (owner_col % NY * SLOT).astype(F32) + slot_col
    from_slot = ones_where((iota((NPIV, NY * SLOT), 1).astype(F32) == source) & (z_col == z)).astype(BF16)
    compact = dot(to_rank, from_slot).astype(BF16)
    target = (z_col * GROUP).astype(F32) + rank_col
    hot[...] = ones_where(iota((NPIV, NZ * GROUP), 1).astype(F32) == target).astype(BF16)

    for b in range(NBLK):
        inv_t[b] = inv[b].T
    rings = (ring_a, ring_b)
    n_coeff, n_early = coeffs.shape[-1], earlier.shape[-1]
    for copy in fetch:
        copy.wait()
    sel[:, :n_coeff] = dot(pick, coeffs[...].reshape(1024, n_coeff)).astype(BF16)
    sel[:, n_coeff:n_coeff + n_early] = dot(pick, earlier[...].reshape(1024, n_early)).astype(BF16)
    rest = NY * QCOL - n_coeff - n_early
    sel[:, n_coeff + n_early:] = jnp.zeros((SLOT, rest), BF16)

    pl.semaphore_wait(barrier, len(peers))

    def quarter(v):
        return pl.ds(pl.multiple_of(v * QCOL, 128), QCOL)

    spread = [remote(sel.at[:, quarter(v)], ygot.at[y], y1s.at[i], y1r.at[i], at(yy=v)) for i, v in enumerate(ys)]
    start(spread)
    sent += spread
    ygot[y] = sel[:, quarter(y)]
    arrive(spread)
    chunk = dot(compact, ygot[...].reshape(NY * SLOT, QCOL)).astype(BF16)

    def chunk_rows(v):
        return pl.ds(pl.multiple_of(v * GROUP, 16), GROUP)

    for g, (low_col, width) in enumerate(PARTS):
        rings[g][chunk_rows(z), :] = chunk[:, low_col:low_col + width]

    def ring_copy(way, step, g, far):
        sign = 1 if way == 0 else NZ - 1
        origin = (z + (NZ - sign) * 2 * (step - 1)) % NZ
        ref = rings[g].at[chunk_rows(origin), :]
        return remote(ref, ref, zs.at[way, step - 1, g, far], zr.at[way, step - 1, g, far],
                      at(zz=(z + sign * (1 + far)) % NZ))

    hops = {}
    for g in range(len(PARTS)):
        for way in (0, 1):
            for step in range(1, STEPS + 1):
                hops[way, step, g, 0] = ring_copy(way, step, g, 0)
                if step < STEPS or way == g % 2:
                    hops[way, step, g, 1] = ring_copy(way, step, g, 1)
    sent += list(hops.values())

    def columns(v, g):
        return pl.ds(pl.multiple_of(v * QCOL + PARTS[g][0], 128), PARTS[g][1])

    def ring_tick(tick):
        for g in range(len(PARTS)):
            step = tick - LAG[g]
            for way in (0, 1):
                if 1 < step <= STEPS:
                    hops[way, step - 1, g, 1].wait_recv()
                for far in (1, 0):
                    if (way, step, g, far) in hops:
                        hops[way, step, g, far].start()

    def gathered(g):
        for (way, step, gg, far), copy in hops.items():
            if gg == g and (far == 0 or step == STEPS):
                copy.wait_recv()
        rows[:, columns(y, g)] = dot(hot[...], rings[g][...]).astype(BF16)

    for tick in range(1, STEPS + LAG[1] + 1):
        ring_tick(tick)
    last_width = n_coeff + n_early - (NY - 1) * QCOL
    n_chunk = NPIV // CHUNK

    def y_copies(q, width):
        ref = rows.at[pl.ds(q * CHUNK, CHUNK), pl.ds(pl.multiple_of(y * QCOL, 128), width)]
        return [remote(ref, ref, y2s.at[q, i], y2r.at[q, i], at(yy=v)) for i, v in enumerate(ys)]

    def by_width(from_y, act):
        @pl.when(from_y != NY - 1)
        def _():
            act(QCOL)

        @pl.when(from_y == NY - 1)
        def _():
            act(last_width)

    def y_send(q):
        by_width(y, lambda width: start(y_copies(q, width)))

    def y_sent(q):
        by_width(y, lambda width: [copy.wait_send() for copy in y_copies(q, width)])

    def y_arrive(q):
        for i, d in enumerate((1, 3, 2)):
            by_width((y + NY - d) % NY, lambda width: y_copies(q, width)[i].wait_recv())
        if q + WINDOW < n_chunk:
            y_send(q + WINDOW)

    gathered(0)
    gathered(1)
    for q in range(WINDOW):
        y_send(q)

    mine = rows[:, quarter(y)]
    gain = jnp.where(y == NY - 1, -1.0, 1.0).astype(F32)
    for b in (1, 2, 3):
        value = dot_nt(mine[b * BLK:(b + 1) * BLK], mine[:b * BLK]) * gain
        for c in range(b):
            diag[LOW.index((b, c))] = value[:, c * BLK:(c + 1) * BLK]
    d1 = remote(diag.at[pl.ds(other * 3, 3)], diag_core, d1s, d1r, at(cc=other))
    d1.start()

    def few_rows(v):
        return pl.ds(pl.multiple_of(v * 32, 32), 32)

    d1.wait_recv()
    diag_sum[...] = diag[pl.ds(core * 3, 3)] + diag_core[...]
    d2 = [remote(diag_sum.at[:, few_rows(v)], diag_x.at[x], d2s.at[i], d2r.at[i], at(xx=v)) for i, v in enumerate(xs)]
    start(d2)
    diag_x[x] = diag_sum[:, few_rows(x)]
    sent += [d1] + d2

    def density(b, c):
        block = rows[b * BLK:(b + 1) * BLK, :]
        left = dot_nt(coeffs[:, c].reshape(NX * BLK, n_coeff), block[:, :n_coeff])
        return left - dot_nt(earlier[:, c].reshape(NX * BLK, n_early), block[:, n_coeff:n_coeff + n_early])

    core_copies = []

    def to_core(b):
        for q in range(b * BLK // CHUNK, (b + 1) * BLK // CHUNK):
            y_arrive(q)
        part_send[b] = density(b, other)
        copy = remote(part_send.at[b], part_got.at[b], pcs.at[b], pcr.at[b], at(cc=other))
        copy.start()
        core_copies.append(copy)
        part_sum[b] = density(b, core)

    def chip(v):
        return pl.ds(pl.multiple_of(v * BLK, BLK), BLK)

    x_copies = []

    def to_x(b):
        core_copies[b].wait_recv()
        part_sum[b] = part_sum[b] + part_got[b]
        copies = [remote(part_sum.at[b, chip(v)], x_got.at[b, i], xas.at[b, i], xar.at[b, i], at(xx=v))
                  for i, v in enumerate(xs)]
        start(copies)
        x_copies.append(copies)

    low = {}
    new = []
    home = [(x, other)] + [(v, c) for v in xs for c in (core, other)]
    less = {}

    def finish(b):
        arrive(x_copies[b])
        rest_rows = (part_sum[b, chip(x)] + x_got[b, 0] + x_got[b, 1] + x_got[b, 2]).T
        for d in range(b):
            rest_rows = rest_rows - less[d][(b - d - 1) * BLK:(b - d) * BLK]
        value = dot(inv_t[b], rest_rows, HIGH)
        if b in low:
            less[b] = dot(low[b], value, HIGH)
        new.append(value)
        made[b] = value
        for c in (0, 1):
            @pl.when((x != b) | (core != c))
            def _():
                out_copy(b, c).start()

            @pl.when((x == b) & (core == c))
            def _():
                own_copy(b, c).start()

    def own_copy(b, c):
        return pltpu.make_async_copy(made.at[b, pl.ds(c * 64, 64)], out.at[:, chip(narrow)], ins.at[2])

    def out_copy(b, c):
        return remote(made.at[b, pl.ds(c * 64, 64)], out.at[:, chip(narrow)], os_.at[b, c], or_.at[narrow], at(xx=b, cc=c))

    to_core(0)
    arrive(d2)
    diag_y[y] = diag_x[0] + diag_x[1] + diag_x[2] + diag_x[3]
    d3 = [remote(diag_y.at[y], diag_y.at[y], d3s.at[i], d3r.at[i], at(yy=v)) for i, v in enumerate(ys)]
    start(d3)
    to_x(0)
    to_core(1)
    to_x(1)
    arrive(d3)
    diag_all[pl.ds(core * 3, 3), few_rows(x)] = diag_y[0] + diag_y[1] + diag_y[2] + diag_y[3]
    spot = diag_all.at[pl.ds(core * 3, 3), few_rows(x)]
    d4 = [remote(spot, spot, d4s.at[i], d4r.at[i], at(xx=v)) for i, v in enumerate(xs)]
    start(d4)
    to_core(2)
    to_x(2)
    finish(0)
    arrive(d4)
    half = diag_all.at[pl.ds(core * 3, 3)]
    d5 = remote(half, half, d5s, d5r, at(cc=other))
    d5.start()
    to_core(3)
    to_x(3)
    d5.wait_recv()

    for c in range(3):
        rest_rows = jnp.concatenate([diag_all[LOW.index((b, c))] for b in range(c + 1, NBLK)], axis=0)
        for d in range(c):
            skip = (c - d) * BLK
            rest_rows = rest_rows - dot_nt(low[d][skip:], low[d][skip - BLK:skip], HIGH)
        low[c] = dot(rest_rows, inv[c], HIGH)
    less[0] = dot(low[0], new[0], HIGH)
    for b in (1, 2, 3):
        finish(b)

    for xx, cc in home:
        source_n = xx * 2 + cc
        remote(made.at[0, pl.ds(0, 64)], out.at[:, chip(source_n)], os_.at[0, 0], or_.at[source_n], at(xx=xx, cc=cc)).wait_recv()
    for b in range(NBLK):
        for c in (0, 1):
            @pl.when((x != b) | (core != c))
            def _():
                out_copy(b, c).wait_send()

            @pl.when((x == b) & (core == c))
            def _():
                own_copy(b, c).wait()
    sent += d3 + d4 + [d5] + core_copies
    for q in range(n_chunk):
        y_sent(q)
    for copies in x_copies:
        sent += copies
    for copy in sent:
        copy.wait_send()


def on_device(coeffs, earlier, inv_tiles, piv_local, piv_owner):
    n_coeff, n_early = coeffs.shape[1], earlier.shape[1]
    dma = pltpu.SemaphoreType.DMA
    vmem = pltpu.VMEM
    in_vmem = pl.BlockSpec(memory_space=pltpu.VMEM)
    anywhere = pl.BlockSpec(memory_space=pl.ANY)
    result = pl.pallas_call(
        kernel,
        out_shape=jax.ShapeDtypeStruct((NPIV // (2 * NX), 1024), F32),
        in_specs=[anywhere, anywhere, in_vmem, in_vmem, in_vmem],
        out_specs=anywhere,
        scratch_shapes=[
            vmem((NX, 2, BLK, n_coeff), BF16),
            vmem((NX, 2, BLK, n_early), BF16),
            vmem((NBLK, BLK, BLK), F32),
            vmem((SLOT, NY * QCOL), BF16),
            vmem((NY, SLOT, QCOL), BF16),
            vmem((NZ * GROUP, PARTS[0][1]), BF16),
            vmem((NZ * GROUP, PARTS[1][1]), BF16),
            vmem((NPIV, NY * QCOL), BF16),
            vmem((NPIV, NZ * GROUP), BF16),
            vmem((6, BLK, BLK), F32),
            vmem((3, BLK, BLK), F32),
            vmem((3, BLK, BLK), F32),
            vmem((NX, 3, 32, BLK), F32),
            vmem((NY, 3, 32, BLK), F32),
            vmem((6, BLK, BLK), F32),
            vmem((NBLK, NX * BLK, BLK), F32),
            vmem((NBLK, NX * BLK, BLK), F32),
            vmem((NBLK, NX * BLK, BLK), F32),
            vmem((NBLK, 3, BLK, BLK), F32),
            vmem((NBLK, BLK, BLK), F32),
            dma((3,)),
            dma((3,)), dma((3,)),
            dma((2, STEPS, len(PARTS), 2)), dma((2, STEPS, len(PARTS), 2)),
            dma((NPIV // CHUNK, 3)), dma((NPIV // CHUNK, 3)),
            dma, dma,
            dma((3,)), dma((3,)),
            dma((3,)), dma((3,)),
            dma((3,)), dma((3,)),
            dma, dma,
            dma((NBLK,)), dma((NBLK,)),
            dma((NBLK, 3)), dma((NBLK, 3)),
            dma((NBLK, 2)), dma((2 * NX,)),
        ],
        compiler_params=pltpu.CompilerParams(
            collective_id=0, has_side_effects=True, vmem_limit_bytes=56 * 1024 * 1024),
        cost_estimate=pl.CostEstimate(flops=4_000_000_000, bytes_accessed=4_000_000, transcendentals=0),
    )(coeffs.reshape(NX, 2, BLK, n_coeff), earlier.reshape(NX, 2, BLK, n_early), inv_tiles,
      piv_owner.reshape(1, NPIV), piv_local.reshape(1, NPIV))
    return result.T


def solution(mesh):
    return jax.shard_map(
        on_device,
        mesh=mesh,
        in_specs=(P("wide", "narrow"), P("wide", "narrow"), P(), P(), P()),
        out_specs=P("wide", "narrow"),
        check_vma=False,
    )
```

```python
import jax
import jax.numpy as jnp
from jax import lax
from jax.experimental import pallas as pl
from jax.experimental.pallas import tpu as pltpu
from jax.sharding import PartitionSpec as P

MESH = pl.DeviceIdType.MESH
F32 = jnp.float32
BF16 = jnp.bfloat16
HIGH = lax.Precision.HIGHEST

NPIV = 512
BLK = 128
NBLK = 4
NY = 4
NZ = 16
NX = 4
CAP = 24
SLOT = 32
GROUP = CAP * NY
QCOL = 384
PARTS = ((0, 128), (128, 256))
LAG = (0, 0)
LOW = ((1, 0), (2, 0), (2, 1), (3, 0), (3, 1), (3, 2))
SIZES = (128, 128, 128, 128)
CHUNK = 64
WINDOW = 3
STEPS = NZ // 4


def dot(a, b, precision=None):
    return lax.dot_general(a, b, (((1,), (0,)), ((), ())), precision=precision, preferred_element_type=F32)


def dot_nt(a, b, precision=None):
    return lax.dot_general(a, b, (((1,), (1,)), ((), ())), precision=precision, preferred_element_type=F32)


def ones_where(cond):
    return jnp.where(cond, 1.0, 0.0).astype(F32)


def iota(shape, dim):
    return lax.broadcasted_iota(jnp.int32, shape, dim)


def kernel(coeffs_in, earlier_in, inv, own_row, loc_row, out,
           coeffs, earlier, inv_t, sel, ygot, ring_a, ring_b, rows, hot,
           diag, diag_core, diag_sum, diag_x, diag_y, diag_all,
           part_send, part_got, part_sum, x_got, made,
           ins, y1s, y1r, zs, zr, y2s, y2r, d1s, d1r, d2s, d2r, d3s, d3r, d4s, d4r, d5s, d5r,
           pcs, pcr, xas, xar, os_, or_):
    wide = lax.axis_index("wide")
    narrow = lax.axis_index("narrow")
    z, y = wide // NY, wide % NY
    x, core = narrow // 2, narrow % 2
    other = 1 - core
    ys = [(y + d) % NY for d in (2, 1, 3)]
    xs = [(x + d) % NX for d in (2, 1, 3)]

    def at(zz=z, yy=y, xx=x, cc=core):
        return {"wide": zz * NY + yy, "narrow": xx * 2 + cc}

    def remote(src, dst, send_sem, recv_sem, device):
        return pltpu.make_async_remote_copy(
            src_ref=src, dst_ref=dst, send_sem=send_sem, recv_sem=recv_sem,
            device_id=device, device_id_type=MESH)

    def start(copies):
        for copy in copies:
            copy.start()

    def arrive(copies):
        for copy in copies:
            copy.wait_recv()

    sent = []

    barrier = pltpu.get_barrier_semaphore()
    peers = [at(zz=(z + d) % NZ) for d in (1, 2, NZ - 1, NZ - 2)] + [at(cc=other)]
    peers += [at(yy=v) for v in ys]
    peers += [at(xx=v, cc=c) for v in xs for c in (core, other)]
    for peer in peers:
        pl.semaphore_signal(barrier, inc=1, device_id=peer, device_id_type=MESH)
    fetch = [pltpu.make_async_copy(coeffs_in, coeffs, ins.at[0]), pltpu.make_async_copy(earlier_in, earlier, ins.at[1])]
    start(fetch)

    owners = own_row[...]
    up, along = iota((NPIV, NPIV), 0), iota((NPIV, NPIV), 1)
    owner_col = jnp.sum(jnp.where(up == along, owners.astype(F32), 0.0), axis=1, keepdims=True).astype(jnp.int32)
    before, after = up < along, along < up
    same_owner = owner_col == owners
    slot_row = jnp.sum(ones_where(before & same_owner), axis=0, keepdims=True)
    held = (iota((SLOT, NPIV), 0).astype(F32) == slot_row) & (owners == wide)
    place = jnp.sum(jnp.where(held, loc_row[...].astype(F32) + 1.0, 0.0), axis=1, keepdims=True) - 1.0
    pick = ones_where(iota((SLOT, 1024), 1).astype(F32) == place).astype(BF16)

    z_row, z_col = owners // NY, owner_col // NY
    same_z = z_col == z_row
    rank_row = jnp.sum(ones_where(before & same_z), axis=0, keepdims=True)
    rank_col = jnp.sum(ones_where(after & same_z), axis=1, keepdims=True)
    slot_col = jnp.sum(ones_where(after & same_owner), axis=1, keepdims=True)
    to_rank = ones_where((iota((GROUP, NPIV), 0).astype(F32) == rank_row) & (z_row == z)).astype(BF16)
    source = (owner_col % NY * SLOT).astype(F32) + slot_col
    from_slot = ones_where((iota((NPIV, NY * SLOT), 1).astype(F32) == source) & (z_col == z)).astype(BF16)
    compact = dot(to_rank, from_slot).astype(BF16)
    target = (z_col * GROUP).astype(F32) + rank_col
    hot[...] = ones_where(iota((NPIV, NZ * GROUP), 1).astype(F32) == target).astype(BF16)

    for b in range(NBLK):
        inv_t[b] = inv[b].T
    rings = (ring_a, ring_b)
    n_coeff, n_early = coeffs.shape[-1], earlier.shape[-1]
    for copy in fetch:
        copy.wait()
    sel[:, :n_coeff] = dot(pick, coeffs[...].reshape(1024, n_coeff)).astype(BF16)
    sel[:, n_coeff:n_coeff + n_early] = dot(pick, earlier[...].reshape(1024, n_early)).astype(BF16)
    rest = NY * QCOL - n_coeff - n_early
    sel[:, n_coeff + n_early:] = jnp.zeros((SLOT, rest), BF16)

    pl.semaphore_wait(barrier, len(peers))

    def quarter(v):
        return pl.ds(pl.multiple_of(v * QCOL, 128), QCOL)

    spread = [remote(sel.at[:, quarter(v)], ygot.at[y], y1s.at[i], y1r.at[i], at(yy=v)) for i, v in enumerate(ys)]
    start(spread)
    sent += spread
    ygot[y] = sel[:, quarter(y)]
    arrive(spread)
    chunk = dot(compact, ygot[...].reshape(NY * SLOT, QCOL)).astype(BF16)

    def chunk_rows(v):
        return pl.ds(pl.multiple_of(v * GROUP, 16), GROUP)

    for g, (low_col, width) in enumerate(PARTS):
        rings[g][chunk_rows(z), :] = chunk[:, low_col:low_col + width]

    def ring_copy(way, step, g, far):
        sign = 1 if way == 0 else NZ - 1
        origin = (z + (NZ - sign) * 2 * (step - 1)) % NZ
        ref = rings[g].at[chunk_rows(origin), :]
        return remote(ref, ref, zs.at[way, step - 1, g, far], zr.at[way, step - 1, g, far],
                      at(zz=(z + sign * (1 + far)) % NZ))

    hops = {}
    for g in range(len(PARTS)):
        for way in (0, 1):
            for step in range(1, STEPS + 1):
                hops[way, step, g, 0] = ring_copy(way, step, g, 0)
                if step < STEPS or way == g % 2:
                    hops[way, step, g, 1] = ring_copy(way, step, g, 1)
    sent += list(hops.values())

    def columns(v, g):
        return pl.ds(pl.multiple_of(v * QCOL + PARTS[g][0], 128), PARTS[g][1])

    def ring_tick(tick):
        for g in range(len(PARTS)):
            step = tick - LAG[g]
            for way in (0, 1):
                if 1 < step <= STEPS:
                    hops[way, step - 1, g, 1].wait_recv()
                for far in (1, 0):
                    if (way, step, g, far) in hops:
                        hops[way, step, g, far].start()

    def gathered(g):
        for (way, step, gg, far), copy in hops.items():
            if gg == g and (far == 0 or step == STEPS):
                copy.wait_recv()
        rows[:, columns(y, g)] = dot(hot[...], rings[g][...]).astype(BF16)

    for tick in range(1, STEPS + LAG[1] + 1):
        ring_tick(tick)
    last_width = n_coeff + n_early - (NY - 1) * QCOL
    n_chunk = NPIV // CHUNK

    def y_copies(q, width):
        ref = rows.at[pl.ds(q * CHUNK, CHUNK), pl.ds(pl.multiple_of(y * QCOL, 128), width)]
        return [remote(ref, ref, y2s.at[q, i], y2r.at[q, i], at(yy=v)) for i, v in enumerate(ys)]

    def by_width(from_y, act):
        @pl.when(from_y != NY - 1)
        def _():
            act(QCOL)

        @pl.when(from_y == NY - 1)
        def _():
            act(last_width)

    def y_send(q):
        by_width(y, lambda width: start(y_copies(q, width)))

    def y_sent(q):
        by_width(y, lambda width: [copy.wait_send() for copy in y_copies(q, width)])

    def y_arrive(q):
        for i, d in enumerate((2, 1, 3)):
            by_width((y + NY - d) % NY, lambda width: y_copies(q, width)[i].wait_recv())
        if q + WINDOW < n_chunk:
            y_send(q + WINDOW)

    gathered(0)
    gathered(1)
    for q in range(WINDOW):
        y_send(q)

    mine = rows[:, quarter(y)]
    gain = jnp.where(y == NY - 1, -1.0, 1.0).astype(F32)
    for b in (1, 2, 3):
        value = dot_nt(mine[b * BLK:(b + 1) * BLK], mine[:b * BLK]) * gain
        for c in range(b):
            diag[LOW.index((b, c))] = value[:, c * BLK:(c + 1) * BLK]
    d1 = remote(diag.at[pl.ds(other * 3, 3)], diag_core, d1s, d1r, at(cc=other))
    d1.start()

    def few_rows(v):
        return pl.ds(pl.multiple_of(v * 32, 32), 32)

    d1.wait_recv()
    diag_sum[...] = diag[pl.ds(core * 3, 3)] + diag_core[...]
    d2 = [remote(diag_sum.at[:, few_rows(v)], diag_x.at[x], d2s.at[i], d2r.at[i], at(xx=v)) for i, v in enumerate(xs)]
    start(d2)
    diag_x[x] = diag_sum[:, few_rows(x)]
    sent += [d1] + d2

    starts = [sum(SIZES[:k]) for k in range(len(SIZES) + 1)]

    def span(k):
        return pl.ds(starts[k], SIZES[k])

    def density(k, c):
        block = rows[starts[k]:starts[k + 1], :]
        left = dot_nt(block[:, :n_coeff], coeffs[:, c].reshape(NX * BLK, n_coeff))
        return left - dot_nt(block[:, n_coeff:n_coeff + n_early], earlier[:, c].reshape(NX * BLK, n_early))

    core_copies = []

    def to_core(k):
        for q in range(starts[k] // CHUNK, starts[k + 1] // CHUNK):
            y_arrive(q)
        part_send[span(k)] = density(k, other)
        copy = remote(part_send.at[span(k)], part_got.at[span(k)], pcs.at[k], pcr.at[k], at(cc=other))
        copy.start()
        core_copies.append(copy)
        part_sum[span(k)] = density(k, core)

    def chip(v):
        return pl.ds(pl.multiple_of(v * BLK, BLK), BLK)

    x_copies = []

    def to_x(k):
        core_copies[k].wait_recv()
        part_sum[span(k)] = part_sum[span(k)] + part_got[span(k)]
        copies = [remote(part_sum.at[span(k), chip(v)], x_got.at[i, span(k)], xas.at[k, i], xar.at[k, i], at(xx=v))
                  for i, v in enumerate(xs)]
        start(copies)
        x_copies.append(copies)

    low = {}
    new = []
    home = [(x, other)] + [(v, c) for v in xs for c in (core, other)]
    less = {}

    def finish(b):
        for k in range(len(SIZES)):
            if b * BLK <= starts[k] < (b + 1) * BLK:
                arrive(x_copies[k])
        block = pl.ds(b * BLK, BLK)
        rest_rows = part_sum[block, chip(x)] + x_got[0, block] + x_got[1, block] + x_got[2, block]
        for d in range(b):
            rest_rows = rest_rows - less[d][(b - d - 1) * BLK:(b - d) * BLK]
        value = dot(inv_t[b], rest_rows, HIGH)
        if b in low:
            less[b] = dot(low[b], value, HIGH)
        new.append(value)
        made[b] = value
        for c in (0, 1):
            @pl.when((x != b) | (core != c))
            def _():
                out_copy(b, c).start()

            @pl.when((x == b) & (core == c))
            def _():
                own_copy(b, c).start()

    def own_copy(b, c):
        return pltpu.make_async_copy(made.at[b, pl.ds(c * 64, 64)], out.at[:, chip(narrow)], ins.at[2])

    def out_copy(b, c):
        return remote(made.at[b, pl.ds(c * 64, 64)], out.at[:, chip(narrow)], os_.at[b, c], or_.at[narrow], at(xx=b, cc=c))

    to_core(0)
    arrive(d2)
    diag_y[y] = diag_x[0] + diag_x[1] + diag_x[2] + diag_x[3]
    d3 = [remote(diag_y.at[y], diag_y.at[y], d3s.at[i], d3r.at[i], at(yy=v)) for i, v in enumerate(ys)]
    start(d3)
    to_x(0)
    to_core(1)
    to_x(1)
    arrive(d3)
    diag_all[pl.ds(core * 3, 3), few_rows(x)] = diag_y[0] + diag_y[1] + diag_y[2] + diag_y[3]
    spot = diag_all.at[pl.ds(core * 3, 3), few_rows(x)]
    d4 = [remote(spot, spot, d4s.at[i], d4r.at[i], at(xx=v)) for i, v in enumerate(xs)]
    start(d4)
    to_core(2)
    to_x(2)
    finish(0)
    arrive(d4)
    half = diag_all.at[pl.ds(core * 3, 3)]
    d5 = remote(half, half, d5s, d5r, at(cc=other))
    d5.start()
    for k in range(3, len(SIZES)):
        to_core(k)
        to_x(k)
    d5.wait_recv()

    for c in range(3):
        rest_rows = jnp.concatenate([diag_all[LOW.index((b, c))] for b in range(c + 1, NBLK)], axis=0)
        for d in range(c):
            skip = (c - d) * BLK
            rest_rows = rest_rows - dot_nt(low[d][skip:], low[d][skip - BLK:skip], HIGH)
        low[c] = dot(rest_rows, inv[c], HIGH)
    less[0] = dot(low[0], new[0], HIGH)
    for b in (1, 2, 3):
        finish(b)

    for xx, cc in home:
        source_n = xx * 2 + cc
        remote(made.at[0, pl.ds(0, 64)], out.at[:, chip(source_n)], os_.at[0, 0], or_.at[source_n], at(xx=xx, cc=cc)).wait_recv()
    for b in range(NBLK):
        for c in (0, 1):
            @pl.when((x != b) | (core != c))
            def _():
                out_copy(b, c).wait_send()

            @pl.when((x == b) & (core == c))
            def _():
                own_copy(b, c).wait()
    sent += d3 + d4 + [d5] + core_copies
    for q in range(n_chunk):
        y_sent(q)
    for copies in x_copies:
        sent += copies
    for copy in sent:
        copy.wait_send()


def on_device(coeffs, earlier, inv_tiles, piv_local, piv_owner):
    n_coeff, n_early = coeffs.shape[1], earlier.shape[1]
    dma = pltpu.SemaphoreType.DMA
    vmem = pltpu.VMEM
    in_vmem = pl.BlockSpec(memory_space=pltpu.VMEM)
    anywhere = pl.BlockSpec(memory_space=pl.ANY)
    result = pl.pallas_call(
        kernel,
        out_shape=jax.ShapeDtypeStruct((NPIV // (2 * NX), 1024), F32),
        in_specs=[anywhere, anywhere, in_vmem, in_vmem, in_vmem],
        out_specs=anywhere,
        scratch_shapes=[
            vmem((NX, 2, BLK, n_coeff), BF16),
            vmem((NX, 2, BLK, n_early), BF16),
            vmem((NBLK, BLK, BLK), F32),
            vmem((SLOT, NY * QCOL), BF16),
            vmem((NY, SLOT, QCOL), BF16),
            vmem((NZ * GROUP, PARTS[0][1]), BF16),
            vmem((NZ * GROUP, PARTS[1][1]), BF16),
            vmem((NPIV, NY * QCOL), BF16),
            vmem((NPIV, NZ * GROUP), BF16),
            vmem((6, BLK, BLK), F32),
            vmem((3, BLK, BLK), F32),
            vmem((3, BLK, BLK), F32),
            vmem((NX, 3, 32, BLK), F32),
            vmem((NY, 3, 32, BLK), F32),
            vmem((6, BLK, BLK), F32),
            vmem((NPIV, NX * BLK), F32),
            vmem((NPIV, NX * BLK), F32),
            vmem((NPIV, NX * BLK), F32),
            vmem((3, NPIV, BLK), F32),
            vmem((NBLK, BLK, BLK), F32),
            dma((3,)),
            dma((3,)), dma((3,)),
            dma((2, STEPS, len(PARTS), 2)), dma((2, STEPS, len(PARTS), 2)),
            dma((NPIV // CHUNK, 3)), dma((NPIV // CHUNK, 3)),
            dma, dma,
            dma((3,)), dma((3,)),
            dma((3,)), dma((3,)),
            dma((3,)), dma((3,)),
            dma, dma,
            dma((len(SIZES),)), dma((len(SIZES),)),
            dma((len(SIZES), 3)), dma((len(SIZES), 3)),
            dma((NBLK, 2)), dma((2 * NX,)),
        ],
        compiler_params=pltpu.CompilerParams(
            collective_id=0, has_side_effects=True, vmem_limit_bytes=56 * 1024 * 1024),
        cost_estimate=pl.CostEstimate(flops=4_000_000_000, bytes_accessed=4_000_000, transcendentals=0),
    )(coeffs.reshape(NX, 2, BLK, n_coeff), earlier.reshape(NX, 2, BLK, n_early), inv_tiles,
      piv_owner.reshape(1, NPIV), piv_local.reshape(1, NPIV))
    return result.T


def solution(mesh):
    return jax.shard_map(
        on_device,
        mesh=mesh,
        in_specs=(P("wide", "narrow"), P("wide", "narrow"), P(), P(), P()),
        out_specs=P("wide", "narrow"),
        check_vma=False,
    )
```
